32 devices in a mesh: tile: 4 (over z), focus: 8 (over y, x, core).
Axes of the slice: x: 2, y: 2, z: 4, core: 2. Of those that a mesh axis runs over, the one named last changes fastest.
Arguments:
- mask_tiles: bfloat16 [256, 512, 512], P(('tile', 'focus')), may hold values from -1 to 1
- class_of_tile: int32 [256, 1], P(('tile', 'focus')), may hold values from 0 to 7; in each aligned block of 8 rows (0 to 7, 8 to 15, ...) at most 2 rows name the same one
- cell_of_tile: int32 [256], P(('tile', 'focus')), may hold values from 0 to 511
- kernels: bfloat16 [8, 24, 4, 4096], P('focus'), may hold values from -0.19921875 to 0.19921875
- class_center: float32 [8], replicated, may hold values from -0.6 to 0.6
Outputs:
- resist_image: bfloat16 [256, 512, 512], P(('tile', 'focus'))
The draws below stay inside these ranges and needn't reach their ends.
Inputs may be any that keep to these rules, and one draw needn't show every extreme that they name: `class_of_tile`: the 8 tiles of one device hold at most 2 tiles of any one class.
All inputs are finite; a program needn't handle non-finite values.
Results may differ from the reference program's by a relative error of at most 0.009.
Values may be sent and summed in bfloat16 or wider, within the bound.
A program may use at most 128 MiB of HBM per device.

```python
import math
import jax
import jax.numpy as jnp
import numpy as np
from jax import lax

P_SIZE = 512
NF = 64
KER = 24
BLK_PX = 64
CAP = 2
SC = 32
TILE_DEV = 8
Q = 128
B = 8
SETS = 8
TILES = 256
NSUP = 512
REACH = 64


def draw_mask_tiles(key, part):
    scale_key, value_key = jax.random.split(jax.random.fold_in(key, 11))
    levels = jnp.exp(jax.random.uniform(scale_key, (TILES, B, B), jnp.float32, jnp.log(0.1), 0.0))
    levels = jnp.repeat(jnp.repeat(levels, BLK_PX, axis=1), BLK_PX, axis=2)
    values = jax.random.uniform(value_key, (TILES, P_SIZE, P_SIZE), jnp.float32, -1.0, 1.0)
    return (levels * values).astype(jnp.bfloat16)


def set_ends(entries, key, least, largest):
    index_at = [jax.random.randint(jax.random.fold_in(key, axis), (), 0, length) for axis, length in enumerate(entries.shape)]
    main_axis = entries.shape.index(max(entries.shape))
    neighbour = index_at[:main_axis] + [(index_at[main_axis] + 1) % entries.shape[main_axis]] + index_at[main_axis + 1:]
    return entries.at[tuple(index_at)].set(least).at[tuple(neighbour)].set(largest)


def block_levels(rng, dims, cuts, low, high):
    loudness, own = 1.0, jax.random.fold_in(rng, 6)
    for dim, blocks in cuts:
        steps = jnp.exp(jax.random.uniform(jax.random.fold_in(own, dim), (blocks,), jnp.float32, low / len(cuts), high / len(cuts)))
        loudness = loudness * jnp.repeat(steps, dims[dim] // blocks).reshape([-1 if axis == dim else 1 for axis in range(len(dims))])
    return loudness


def shared_out(rng, own, number, rows, number_of, top, bound, lean):
    order = jax.random.permutation(rng, number_of)
    crowded, usual = portions_of(number_of, rows * top, bound, lean, True), portions_of(number_of, rows * top, bound, lean, False)
    places = jnp.arange(number_of)

    def named(tallies, offset_by):
        used = int((tallies > 0).sum())
        fixed = max(1, used // 4)
        moved = fixed + (places - fixed + offset_by * (used - fixed)) % max(1, number_of - fixed)
        return jnp.zeros((number_of,), jnp.int32).at[order[jnp.where(places < fixed, places, moved)]].set(jnp.asarray(tallies, jnp.int32))

    tallies = jnp.where(number % 4 == 0, named(crowded, number // 4), named(usual, number - number // 4 - 1))
    mixed = jax.random.permutation(jax.random.fold_in(own, 3), number_of)
    donor, receiver = mixed[0:number_of // 2 * 2:2], mixed[1:number_of // 2 * 2:2]
    room = jnp.minimum(tallies[donor] - 1, bound - tallies[receiver]) // 2
    room = jnp.where((donor == order[0]) | (receiver == order[0]) | (tallies[receiver] == 0), 0, jnp.maximum(room, 0))
    moved = jax.random.randint(jax.random.fold_in(own, 4), (number_of // 2,), 0, 1 << 20) % (room + 1)
    tallies = tallies.at[donor].add(-moved).at[receiver].add(moved)
    labels = jnp.searchsorted(jnp.cumsum(tallies), jnp.arange(rows * top), side="right").astype(jnp.int32)
    listing = labels.reshape(top, rows).T
    listing = listing[jax.random.permutation(jax.random.fold_in(own, 1), rows)]
    offset_by = jax.random.randint(jax.random.fold_in(own, 2), (rows, 1), 0, top)
    return jnp.take_along_axis(listing, (jnp.arange(top)[None, :] + offset_by) % top, axis=1)


def portions_of(number_of, total, bound, lean, full):
    weights = [(1 << 20) // math.isqrt(grade ** lean) + 1 for grade in range(1, number_of + 1)]
    largest = bound if full else min(bound, max(-(-total // number_of), total * weights[0] // sum(weights)))
    least = 1 if total - largest >= number_of - 1 else 0
    holding, spare = [largest] + [least] * (number_of - 1), total - largest - least * (number_of - 1)
    while spare > 0:
        candidates = [i for i in range(1, number_of) if holding[i] < largest] or [i for i in range(1, number_of) if holding[i] < bound]
        whole, budget = sum([weights[i] for i in candidates]), spare
        for i in candidates:
            addition = min(bound - holding[i], max(1, budget * weights[i] // whole), spare)
            holding[i] = holding[i] + addition
            spare = spare - addition
    return np.array(holding)


def gaussian(rng, shape, scale, limit, pieces=(), held_as=jnp.bfloat16):
    drawn = jax.random.normal(rng, shape, jnp.float32) * scale
    if len(pieces) > 0:
        drawn = block_levels(rng, shape, pieces, -0.22, 0.18) * drawn
    return jnp.clip(drawn, min=-limit, max=limit).astype(held_as)


def setup_inputs(seed: int = 0) -> dict:
    splits = jax.random.split(jax.random.key(seed), 6)
    mask_tiles = draw_mask_tiles(jax.random.fold_in(splits[5], 71), 0)
    class_of_tile_keys = jax.random.split(jax.random.fold_in(splits[1], 1), TILES // TILE_DEV)
    class_of_tile_turns = jax.random.permutation(jax.random.fold_in(splits[1], 3), TILES // TILE_DEV)
    class_of_tile = jax.vmap(lambda own, number: shared_out(jax.random.fold_in(splits[1], 2), own, number, TILE_DEV, SETS, 1, CAP, 2))(class_of_tile_keys, class_of_tile_turns).reshape((TILES, 1))
    cell_of_tile = set_ends(jax.random.randint(splits[2], (TILES,), 0, NSUP), jax.random.fold_in(splits[2], 1), 0, NSUP - 1).astype(jnp.int32)
    kernels = gaussian(splits[3], (SETS, KER, 4, NF * NF), 0.03125, 0.19921875, ((0, 8),))
    class_center = jnp.clip(jax.random.uniform(splits[4], (SETS,), jnp.float32, -0.6, 0.6), -0.6, 0.6)
    return dict(mask_tiles=mask_tiles, class_of_tile=class_of_tile, cell_of_tile=cell_of_tile, kernels=kernels, class_center=class_center)


GAIN_SCALE = 50.0
BEST = lax.Precision.HIGHEST


def spectral_table(freq_count, length):
    frequency = jnp.arange(freq_count, dtype=jnp.int32) - freq_count // 2
    places = jnp.arange(length, dtype=jnp.int32)
    phases = jnp.mod(frequency[:, None] * places[None, :], length).astype(jnp.float32) * (2.0 * jnp.pi / length)
    return jnp.cos(phases), jnp.sin(phases)


def imaging_table(freq_count, samples):
    cosine, sine_part = spectral_table(freq_count, samples)
    upper_rows = jnp.concatenate([cosine, sine_part], axis=1)
    lower_rows = jnp.concatenate([-sine_part, cosine], axis=1)
    return jnp.concatenate([upper_rows, lower_rows], axis=0).astype(jnp.bfloat16)


def resist_table(pixels, samples):
    cos_pix, sin_pix = spectral_table(samples, pixels)
    cos_smp, sin_smp = spectral_table(samples, samples)
    frequency = (jnp.arange(samples, dtype=jnp.int32) - samples // 2).astype(jnp.float32)
    weight = jnp.exp(-0.5 * (frequency * (4.0 / samples)) ** 2)
    combined = jnp.dot((cos_pix * weight[:, None]).T, cos_smp, precision=BEST)
    combined = combined + jnp.dot((sin_pix * weight[:, None]).T, sin_smp, precision=BEST)
    return (combined / samples).astype(jnp.bfloat16)


def spread_table(extent, length):
    places = jnp.arange(extent, dtype=jnp.int32).astype(jnp.float32)
    weight = jnp.exp(-jnp.abs(places[:, None] - places[None, :]) / length)
    return weight / jnp.sum(weight, axis=1, keepdims=True)


def to_map(totals):
    strips = totals.shape[0] // SC
    return totals.reshape(strips, SC, B, B).transpose(0, 2, 1, 3).reshape(strips * B, SC * B)


def cell_means(field_map):
    strips = field_map.shape[0] // B
    return jnp.mean(field_map.reshape(strips, B, SC, B), axis=(1, 3)).reshape(strips * SC)


def split_spectrum(raw_spectrum):
    cos_cos = raw_spectrum[..., :NF, :NF]
    cos_sin = raw_spectrum[..., :NF, NF:]
    sin_cos = raw_spectrum[..., NF:, :NF]
    sin_sin = raw_spectrum[..., NF:, NF:]
    real_part = (cos_cos - sin_sin) / P_SIZE
    imag_part = -(cos_sin + sin_cos) / P_SIZE
    stacked = jnp.stack([real_part, imag_part], axis=-3)
    return stacked.reshape(raw_spectrum.shape[:-2] + (2, NF * NF)).astype(jnp.bfloat16)


def image_one(spectrum, defocus, kernel_set, right_table, left_table):
    spec_parts = spectrum.astype(jnp.float32)
    weights = kernel_set.astype(jnp.float32)
    kern_re = weights[:, 0] + defocus * weights[:, 2]
    kern_im = weights[:, 1] + defocus * weights[:, 3]
    prod_re = kern_re * spec_parts[0] - kern_im * spec_parts[1]
    prod_im = kern_re * spec_parts[1] + kern_im * spec_parts[0]
    stacked = jnp.concatenate([prod_re.reshape(KER, NF, NF), prod_im.reshape(KER, NF, NF)], axis=2)
    stacked = stacked.astype(jnp.bfloat16).reshape(KER * NF, 2 * NF)
    across = jnp.dot(stacked, right_table, preferred_element_type=jnp.float32).astype(jnp.bfloat16)
    across = across.reshape(KER, NF, 2 * Q)
    fields = jnp.einsum("pu,kuv->pkv", left_table[:, :NF], across[:, :, :Q], preferred_element_type=jnp.float32)
    fields = fields + jnp.einsum("pu,kuv->pkv", left_table[:, NF:], across[:, :, Q:], preferred_element_type=jnp.float32)
    return jnp.sum((fields * fields).reshape(2, Q, KER, Q), axis=(0, 2)).reshape(Q * Q) / KER


def reference(mask_tiles, class_of_tile, cell_of_tile, kernels, class_center):
    wave_rows = jnp.concatenate(spectral_table(NF, P_SIZE), axis=0).astype(jnp.bfloat16)
    right_table = imaging_table(NF, Q)
    left_table = right_table.T
    resist_rows = resist_table(P_SIZE, Q)

    def forward_tile(single):
        projected = jnp.dot(single, wave_rows.T, preferred_element_type=jnp.float32).astype(jnp.bfloat16)
        raw_spectrum = jnp.dot(wave_rows, projected, preferred_element_type=jnp.float32)
        squares = single.astype(jnp.float32) ** 2
        density = jnp.sum(squares.reshape(B, BLK_PX, B, BLK_PX), axis=(1, 3)) / (BLK_PX * BLK_PX)
        return split_spectrum(raw_spectrum), density.reshape(B * B)

    spectra, density = lax.map(forward_tile, mask_tiles, batch_size=32)
    totals = jax.ops.segment_sum(density, cell_of_tile, num_segments=NSUP)
    density_map = to_map(totals)
    effective = jnp.dot(spread_table(density_map.shape[0], REACH), density_map, precision=BEST)
    effective = jnp.dot(effective, spread_table(density_map.shape[1], REACH), precision=BEST)
    heights = cell_means(effective)
    classes = class_of_tile[:, 0]
    defocus_all = GAIN_SCALE * (heights[cell_of_tile] - jnp.mean(heights)) - class_center[classes]

    def image_tile(inputs):
        spectrum, defocus, set_id = inputs
        intensity = image_one(spectrum, defocus, kernels[set_id], right_table, left_table)
        intensity = intensity.astype(jnp.bfloat16).reshape(Q, Q)
        half_way = jnp.dot(intensity, resist_rows.T, preferred_element_type=jnp.float32).astype(jnp.bfloat16)
        return jnp.dot(resist_rows, half_way, preferred_element_type=jnp.float32).astype(jnp.bfloat16)

    return lax.map(image_tile, (spectra, defocus_all, classes), batch_size=16)
```

```python
import functools

import jax
import jax.numpy as jnp
import ml_dtypes
import numpy as np
from jax import lax
from jax.experimental import pallas as pl
from jax.experimental.pallas import tpu as pltpu
from jax.sharding import PartitionSpec as P

BLK_PX = 64
CAP = 2
SC = 32
SR_DEV = 4
Q = 128
B = 8
REACH = 64
GAIN_SCALE = 50.0
LANES = 128
MESH = pl.DeviceIdType.MESH
F32 = jnp.float32
BF16 = jnp.bfloat16


def trig(freq_count, length):
    frequency = np.arange(freq_count) - freq_count // 2
    phases = np.mod(frequency[:, None] * np.arange(length)[None, :], length) * (2.0 * np.pi / length)
    return np.cos(phases), np.sin(phases)


def as_bf16(table):
    return np.asarray(table, np.float32).astype(ml_dtypes.bfloat16)


def in_columns(table):
    return np.stack(np.split(table, table.shape[1] // LANES, axis=1))


def whole(ref):
    return jnp.concatenate([ref[i] for i in range(ref.shape[0])], axis=1)


def wave_tables(nf, pixels):
    c, s = trig(nf, pixels)
    across = np.concatenate([c, s], axis=0).T
    down = np.concatenate([c[0::2], c[1::2], s[0::2], s[1::2]], axis=0)
    return as_bf16(across), as_bf16(down)


def image_tables(nf):
    c, s = trig(nf, Q)
    zero = np.zeros_like(c)
    right = np.block([[c, s, zero, zero], [zero, zero, c, s], [-s, c, zero, zero], [zero, zero, -s, c]])
    full = np.block([[c, s], [-s, c]]).T
    order = np.concatenate([np.arange(0, nf, 2), nf + np.arange(0, nf, 2), np.arange(1, nf, 2), nf + np.arange(1, nf, 2)])
    return as_bf16(right), as_bf16(full[:, order])


def resist_table(pixels):
    cp, sp = trig(Q, pixels)
    cq, sq = trig(Q, Q)
    frequency = np.arange(Q) - Q // 2
    weight = np.exp(-0.5 * (frequency * (4.0 / Q)) ** 2)[:, None]
    return as_bf16(((cp * weight).T @ cq + (sp * weight).T @ sq) / Q)


def spread_table(extent):
    places = np.arange(extent)
    weight = np.exp(-np.abs(places[:, None] - places[None, :]) / REACH)
    return weight / weight.sum(axis=1, keepdims=True)


def height_tables(strips):
    down = spread_table(strips * B).reshape(strips, B, strips * B).mean(axis=1).T
    down = np.pad(down, ((0, 0), (0, LANES - strips)))
    along = spread_table(SC * B).reshape(SC * B, SC, B).mean(axis=2).reshape(SC, B * SC)
    return down.astype(np.float32), along.astype(np.float32)


def imaging_kernel(
    n_tile, n_focus, strips, ker, nf,
    mask_hbm, class_ref, cell_ref, center_ref, w_ref, wave_x, wave_y, right_ref, left_ref, down_ref, along_ref,
    ret_ref,
    mask_v, sq_v, sp_v, out_v, in_v, hs_v, hr_v, zs_v, zr_v, shift_v, lit_v,
    mask_sem, h_send, h_recv, z_send, z_recv, s_send, s_recv, r_send, r_recv, own_sem,
):
    my_t, my_f = lax.axis_index("tile"), lax.axis_index("focus")
    tiles, px, _ = mask_v.shape
    half = nf // 2

    def ahead(o):
        return lax.rem(my_f + o, n_focus)

    def behind(o):
        return lax.rem(my_f + n_focus - o, n_focus)

    def above(o):
        return lax.rem(my_t + o, n_tile)

    def mask_copy(t):
        return pltpu.make_async_copy(mask_hbm.at[t], mask_v.at[t], mask_sem.at[t])

    for t in range(tiles):
        mask_copy(t).start()
    barrier = pltpu.get_barrier_semaphore()
    for o in range(1, n_focus):
        pl.semaphore_signal(barrier, inc=1, device_id=(my_t, ahead(o)), device_id_type=MESH)
    for o in range(1, n_tile):
        pl.semaphore_signal(barrier, inc=1, device_id=(above(o), my_f), device_id_type=MESH)

    def forward(t, carry):
        mask_copy(t).wait()
        mask = mask_v[t]
        wide = mask.astype(F32)
        sq_v[pl.ds(pl.multiple_of(t * B, B), B), :] = jnp.sum((wide * wide).reshape(B, BLK_PX, px), axis=1)
        projected = jnp.dot(mask, wave_x[...], preferred_element_type=F32).astype(BF16)
        raw = jnp.dot(whole(wave_y), projected, preferred_element_type=F32)
        top, bottom = raw[:nf], pltpu.roll(raw[nf:], nf, 1)
        real, imag = (top - bottom) / px, -(top + bottom) / px
        low = lax.broadcasted_iota(jnp.int32, (half, 2 * nf), 1) < nf
        packed_re = jnp.where(low, real[:half], pltpu.roll(real[half:], nf, 1))
        packed_im = jnp.where(low, pltpu.roll(imag[:half], nf, 1), imag[half:])
        sp_v[t] = jnp.concatenate([packed_re, packed_im], axis=0).astype(BF16)
        return carry

    lax.fori_loop(0, tiles, forward, 0)

    sums = sq_v[...]
    high = sums.astype(BF16)
    rest = (sums - high.astype(F32)).astype(BF16)
    spot = lax.broadcasted_iota(jnp.int32, (px, B * SC), 0) // BLK_PX
    group = lax.broadcasted_iota(jnp.int32, (px, B * SC), 1) // SC
    fold = jnp.where(spot == group, 1.0 / (BLK_PX * BLK_PX), 0.0).astype(BF16)
    both = jnp.dot(jnp.concatenate([high, rest], axis=0), fold, preferred_element_type=F32)
    density = both[: tiles * B] + both[tiles * B :]
    row_of = lax.broadcasted_iota(jnp.int32, (tiles * B, LANES), 0)
    lane_of = lax.broadcasted_iota(jnp.int32, (tiles * B, LANES), 1)
    cell_rows = jnp.zeros((tiles * B, LANES), jnp.int32)
    classes, cells, slots = [], [], []
    for t in range(tiles):
        classes.append(class_ref[t])
        cells.append(cell_ref[t])
        rank = jnp.int32(0)
        for before in range(t):
            rank = rank + jnp.where(classes[before] == classes[t], 1, 0)
        slots.append(classes[t] * CAP + rank)
        cell_rows = jnp.where(row_of // B == t, cells[t], cell_rows)
    strip_rows = cell_rows // SC
    wanted_column = jnp.where(lane_of == cell_rows - strip_rows * SC, 1.0, 0.0)[:, :SC]
    wanted_row = jnp.concatenate(
        [jnp.where(lane_of + first == strip_rows * B + row_of % B, 1.0, 0.0) for first in range(0, strips * B, LANES)],
        axis=1)
    exact = dict(precision=lax.Precision.HIGHEST, preferred_element_type=F32)
    downs = jnp.dot(wanted_row, down_ref[...], **exact)
    alongs = jnp.dot(wanted_column, along_ref[...], **exact)
    share = lax.dot_general(downs, density * alongs, (((0,), (0,)), ((), ())), **exact)[:strips]
    share = share[:, :LANES] + share[:, LANES:]
    share = share + pltpu.roll(share, 2 * SC, 1)
    share = share + pltpu.roll(share, SC, 1)
    row_at = lax.broadcasted_iota(jnp.int32, (tiles, LANES), 0)
    lane_at = lax.broadcasted_iota(jnp.int32, (tiles, LANES), 1)
    info = jnp.zeros((tiles, LANES), F32)
    for t in range(tiles):
        entry = jnp.where(lane_at == 0, cells[t], slots[t]).astype(F32)
        info = jnp.where(row_at == t, entry, info)
    hs_v[:strips] = share
    hs_v[strips:] = info
    hr_v[0] = hs_v[...]

    pl.semaphore_wait(barrier, n_focus - 1 + n_tile - 1)

    def h_copy(o):
        return pltpu.make_async_remote_copy(
            src_ref=hs_v, dst_ref=hr_v.at[o], send_sem=h_send.at[o], recv_sem=h_recv.at[o],
            device_id=(my_t, ahead(o)), device_id_type=MESH)

    def z_copy(o):
        return pltpu.make_async_remote_copy(
            src_ref=zs_v, dst_ref=zr_v.at[o], send_sem=z_send.at[o], recv_sem=z_recv.at[o],
            device_id=(above(o), my_f), device_id_type=MESH)

    def s_copy(o):
        return pltpu.make_async_remote_copy(
            src_ref=out_v.at[o], dst_ref=in_v.at[o], send_sem=s_send.at[o], recv_sem=s_recv.at[o],
            device_id=(my_t, ahead(o)), device_id_type=MESH)

    def r_copy(o):
        return pltpu.make_async_remote_copy(
            src_ref=lit_v.at[o], dst_ref=ret_ref.at[my_f], send_sem=r_send.at[o], recv_sem=r_recv.at[o],
            device_id=(my_t, behind(o)), device_id_type=MESH)

    for o in range(1, n_focus):
        h_copy(o).start()

    slot_tiles = [jnp.full((8, LANES), slots[t], jnp.int32) for t in range(tiles)]
    for o in range(n_focus):
        target = in_v if o == 0 else out_v
        for j in range(CAP):
            name = ahead(o) * CAP + j
            chosen = jnp.zeros((2 * nf // 16, 8, 2 * nf), F32)
            for t in range(tiles):
                chosen = jnp.where((slot_tiles[t] == name)[None], sp_v[t].astype(F32).reshape(chosen.shape), chosen)
            target[o, j] = chosen.reshape(nf, 2 * nf).astype(BF16)
        if o > 0:
            s_copy(o).start()

    for o in range(1, n_focus):
        h_copy(o).wait_recv()
    subtotal = hr_v[0, :strips]
    for o in range(1, n_focus):
        subtotal = subtotal + hr_v[o, :strips]
    zs_v[...] = subtotal
    for o in range(1, n_tile):
        z_copy(o).start()
    for o in range(1, n_tile):
        z_copy(o).wait_recv()
    heights = subtotal
    for o in range(1, n_tile):
        heights = heights + zr_v[o]
    average = jnp.sum(heights, keepdims=True) / (strips * LANES)
    names = hr_v[:, strips:, :].reshape(n_focus * tiles, LANES)
    cell_col, slot_col = names[:, 0:1], names[:, 1:2]
    strip_col = jnp.floor(cell_col / SC)
    column_col = cell_col - strip_col * SC
    picked = jnp.zeros((n_focus * tiles, LANES), F32)
    for r in range(strips):
        picked = jnp.where(strip_col == r, heights[r : r + 1], picked)
    lane = lax.broadcasted_iota(jnp.int32, picked.shape, 1).astype(F32)
    own = jnp.sum(jnp.where(lane == column_col, picked, 0.0), axis=1, keepdims=True)
    defocus = GAIN_SCALE * (own - average) - center_ref[my_f]
    for j in range(CAP):
        here = slot_col == (my_f * CAP + j).astype(F32)
        kept = jnp.broadcast_to(jnp.where(here, defocus, 0.0), picked.shape)
        shift_v[j] = jnp.sum(kept.reshape(n_focus, tiles, LANES), axis=1)

    def image(o, j):
        d = shift_v[j, pl.ds(o, 1), :]
        spec = in_v[o, j].astype(F32)
        sr, si = spec[:half][None], spec[half:][None]
        w = [w_ref[:, i].astype(F32) for i in range(4)]
        kr, ki = w[0] + d[None] * w[2], w[1] + d[None] * w[3]
        pr = (kr * sr - ki * si).astype(BF16).reshape(ker * half, 2 * nf)
        pi = (kr * si + ki * sr).astype(BF16).reshape(ker * half, 2 * nf)
        across = jnp.dot(jnp.concatenate([pr, pi], axis=1), whole(right_ref), preferred_element_type=F32).astype(BF16)
        left = left_ref[...]
        total = jnp.zeros((Q, Q), F32)
        for k in range(0, ker, 2):
            sides = []
            for m in (k, k + 1):
                rows = across[m * half : (m + 1) * half]
                sides.append(jnp.concatenate([rows[:, i * Q : (i + 1) * Q] for i in range(4)], axis=0))
            fields = jnp.dot(left, jnp.concatenate(sides, axis=1), preferred_element_type=F32)
            power = fields * fields
            total = total + ((power[:Q, :Q] + power[Q:, :Q]) + (power[:Q, Q:] + power[Q:, Q:]))
        return (total / ker).astype(BF16)

    own_copy = pltpu.make_async_copy(lit_v.at[0], ret_ref.at[my_f], own_sem)
    for j in range(CAP):
        lit_v[0, j] = image(0, j)
    own_copy.start()

    def serve(o, carry):
        s_copy(o).wait_recv()
        for j in range(CAP):
            lit_v[o, j] = image(o, j)
        r_copy(o).start()
        return carry

    lax.fori_loop(1, n_focus, serve, 0)
    own_copy.wait()
    for o in range(1, n_focus):
        r_copy(o).wait_recv()
    for o in range(1, n_focus):
        h_copy(o).wait_send()
        s_copy(o).wait_send()
        r_copy(o).wait_send()
    for o in range(1, n_tile):
        z_copy(o).wait_send()


def resist_kernel(per, class_ref, lit_ref, wide_ref, tall_ref, out_ref):
    first = pl.program_id(0) * per
    for i in range(per):
        t = first + i
        own = class_ref[t]
        rank = lax.fori_loop(0, t, lambda b, r: r + jnp.where(class_ref[b] == own, 1, 0), jnp.int32(0))
        light = lit_ref[own * CAP + rank]
        half_way = jnp.dot(light, whole(wide_ref), preferred_element_type=F32).astype(BF16)
        out_ref[i] = jnp.dot(tall_ref[...], half_way, preferred_element_type=F32).astype(BF16)


def per_device(n_tile, n_focus, mask_tiles, class_of_tile, cell_of_tile, kernels, class_center):
    tiles, px, _ = mask_tiles.shape
    _, ker, parts, area = kernels.shape
    nf = int(round(area ** 0.5))
    half = nf // 2
    strips = SR_DEV * n_tile
    wave_x, wave_y = wave_tables(nf, px)
    right, left = image_tables(nf)
    down, along = height_tables(strips)
    resist = resist_table(px)
    weights = kernels.reshape(ker, parts, half, 2 * nf)
    classes = class_of_tile.reshape(tiles)
    smem = pl.BlockSpec(memory_space=pltpu.SMEM)
    vmem = pl.BlockSpec(memory_space=pltpu.VMEM)
    anywhere = pl.BlockSpec(memory_space=pl.ANY)
    dma = pltpu.SemaphoreType.DMA
    slots = n_focus * CAP
    row_work = slots * ker * (half * 4 * nf * 4 * Q + 2 * Q * 2 * nf * Q)
    returned = pl.pallas_call(
        functools.partial(imaging_kernel, n_tile, n_focus, strips, ker, nf),
        out_shape=jax.ShapeDtypeStruct((n_focus, CAP, Q, Q), BF16),
        in_specs=[anywhere, smem, smem, smem] + [vmem] * 7,
        out_specs=anywhere,
        scratch_shapes=[
            pltpu.VMEM((tiles, px, px), BF16),
            pltpu.VMEM((tiles * B, px), F32),
            pltpu.VMEM((tiles, nf, 2 * nf), BF16),
            pltpu.VMEM((n_focus, CAP, nf, 2 * nf), BF16),
            pltpu.VMEM((n_focus, CAP, nf, 2 * nf), BF16),
            pltpu.VMEM((strips + tiles, LANES), F32),
            pltpu.VMEM((n_focus, strips + tiles, LANES), F32),
            pltpu.VMEM((strips, LANES), F32),
            pltpu.VMEM((n_tile, strips, LANES), F32),
            pltpu.VMEM((CAP, n_focus, LANES), F32),
            pltpu.VMEM((n_focus, CAP, Q, Q), BF16),
            dma((tiles,)),
            dma((n_focus,)), dma((n_focus,)),
            dma((n_tile,)), dma((n_tile,)),
            dma((n_focus,)), dma((n_focus,)),
            dma((n_focus,)), dma((n_focus,)),
            dma,
        ],
        compiler_params=pltpu.CompilerParams(
            collective_id=0, has_side_effects=True, vmem_limit_bytes=56 * 1024 * 1024),
        cost_estimate=pl.CostEstimate(flops=2 * row_work, bytes_accessed=8 * 1024 * 1024, transcendentals=0),
        name="imaging",
    )(mask_tiles, classes, cell_of_tile, class_center, weights, wave_x, in_columns(wave_y), in_columns(right), left, down, along)
    per = 2 if tiles % 2 == 0 else 1
    return pl.pallas_call(
        functools.partial(resist_kernel, per),
        out_shape=jax.ShapeDtypeStruct((tiles, px, px), BF16),
        grid=(tiles // per,),
        in_specs=[smem, vmem, vmem, vmem],
        out_specs=pl.BlockSpec((per, px, px), lambda i: (i, 0, 0)),
        compiler_params=pltpu.CompilerParams(vmem_limit_bytes=48 * 1024 * 1024),
        cost_estimate=pl.CostEstimate(
            flops=2 * tiles * Q * px * (Q + px), bytes_accessed=2 * tiles * px * px, transcendentals=0),
        name="resist",
    )(classes, returned.reshape(slots, Q, Q), in_columns(resist.T), resist)


def solution(mesh):
    placed = (
        P(("tile", "focus"), None, None),
        P(("tile", "focus"), None),
        P(("tile", "focus")),
        P("focus", None, None, None),
        P(),
    )
    return jax.shard_map(
        functools.partial(per_device, mesh.shape["tile"], mesh.shape["focus"]),
        mesh=mesh,
        in_specs=placed,
        out_specs=P(("tile", "focus"), None, None),
        check_vma=False,
    )
```

```python
import functools

import jax
import jax.numpy as jnp
import ml_dtypes
import numpy as np
from jax import lax
from jax.experimental import pallas as pl
from jax.experimental.pallas import tpu as pltpu
from jax.sharding import PartitionSpec as P

BLK_PX = 64
CAP = 2
SC = 32
SR_DEV = 4
Q = 128
B = 8
REACH = 64
GAIN_SCALE = 50.0
LANES = 128
MESH = pl.DeviceIdType.MESH
F32 = jnp.float32
BF16 = jnp.bfloat16


def trig(freq_count, length):
    frequency = np.arange(freq_count) - freq_count // 2
    phases = np.mod(frequency[:, None] * np.arange(length)[None, :], length) * (2.0 * np.pi / length)
    return np.cos(phases), np.sin(phases)


def as_bf16(table):
    return np.asarray(table, np.float32).astype(ml_dtypes.bfloat16)


def in_columns(table):
    return np.stack(np.split(table, table.shape[1] // LANES, axis=1))


def whole(ref):
    return jnp.concatenate([ref[i] for i in range(ref.shape[0])], axis=1)


def wave_tables(nf, pixels):
    c, s = trig(nf, pixels)
    across = np.concatenate([c, s], axis=0).T
    down = np.concatenate([c[0::2], c[1::2], s[0::2], s[1::2]], axis=0)
    return as_bf16(across), as_bf16(down)


def image_tables(nf):
    c, s = trig(nf, Q)
    zero = np.zeros_like(c)
    right = np.block([[c, s, zero, zero], [zero, zero, c, s], [-s, c, zero, zero], [zero, zero, -s, c]])
    full = np.block([[c, s], [-s, c]]).T
    order = np.concatenate([np.arange(0, nf, 2), nf + np.arange(0, nf, 2), np.arange(1, nf, 2), nf + np.arange(1, nf, 2)])
    return as_bf16(right), as_bf16(full[:, order])


def resist_table(pixels):
    cp, sp = trig(Q, pixels)
    cq, sq = trig(Q, Q)
    frequency = np.arange(Q) - Q // 2
    weight = np.exp(-0.5 * (frequency * (4.0 / Q)) ** 2)[:, None]
    return as_bf16(((cp * weight).T @ cq + (sp * weight).T @ sq) / Q)


def spread_table(extent):
    places = np.arange(extent)
    weight = np.exp(-np.abs(places[:, None] - places[None, :]) / REACH)
    return weight / weight.sum(axis=1, keepdims=True)


def height_tables(strips):
    down = spread_table(strips * B).reshape(strips, B, strips * B).mean(axis=1).T
    down = np.pad(down, ((0, 0), (0, LANES - strips)))
    along = spread_table(SC * B).reshape(SC * B, SC, B).mean(axis=2).reshape(SC, B * SC)
    return down.astype(np.float32), along.astype(np.float32)


def imaging_kernel(
    n_tile, n_focus, strips, ker, nf,
    mask_hbm, class_ref, cell_ref, center_ref, w_hbm, wave_x_hbm, wave_y_hbm, right_hbm, left_hbm, down_hbm, along_hbm,
    ret_ref,
    mask_v, sq_v, sp_v, out_v, in_v, hs_v, hr_v, zs_v, zr_v, shift_v, lit_v, raw_v, w_v, fil_v,
    wave_x, wave_y, right_ref, left_ref, down_ref, along_ref,
    mask_sem, h_send, h_recv, z_send, z_recv, s_send, s_recv, r_send, r_recv, own_sem, table_sem,
):
    my_t, my_f = lax.axis_index("tile"), lax.axis_index("focus")
    tiles, px, _ = mask_v.shape
    half = nf // 2

    def ahead(o):
        return lax.rem(my_f + o, n_focus)

    def behind(o):
        return lax.rem(my_f + n_focus - o, n_focus)

    def above(o):
        return lax.rem(my_t + o, n_tile)

    def mask_copy(t):
        return pltpu.make_async_copy(mask_hbm.at[t], mask_v.at[t], mask_sem.at[t])

    fetched = [
        (down_hbm, down_ref), (along_hbm, along_ref), (wave_x_hbm, wave_x), (wave_y_hbm, wave_y),
        (w_hbm.at[0], raw_v), (right_hbm, right_ref), (left_hbm, left_ref)]
    tables = [pltpu.make_async_copy(src, dst, table_sem.at[i]) for i, (src, dst) in enumerate(fetched)]

    for t in range(tiles):
        mask_copy(t).start()
    for table in tables:
        table.start()
    barrier = pltpu.get_barrier_semaphore()
    for o in range(1, n_focus):
        pl.semaphore_signal(barrier, inc=1, device_id=(my_t, ahead(o)), device_id_type=MESH)
    for o in range(1, n_tile):
        pl.semaphore_signal(barrier, inc=1, device_id=(above(o), my_f), device_id_type=MESH)

    def squares(t, carry):
        mask_copy(t).wait()
        wide = mask_v[t].astype(F32)
        sq_v[pl.ds(pl.multiple_of(t * B, B), B), :] = jnp.sum((wide * wide).reshape(B, BLK_PX, px), axis=1)
        return carry

    lax.fori_loop(0, tiles, squares, 0)
    tables[0].wait()
    tables[1].wait()

    def spectrum(t):
        projected = jnp.dot(mask_v[t], wave_x[...], preferred_element_type=F32).astype(BF16)
        raw = jnp.dot(whole(wave_y), projected, preferred_element_type=F32)
        top, bottom = raw[:nf], pltpu.roll(raw[nf:], nf, 1)
        real, imag = (top - bottom) / px, -(top + bottom) / px
        low = lax.broadcasted_iota(jnp.int32, (half, 2 * nf), 1) < nf
        packed_re = jnp.where(low, real[:half], pltpu.roll(real[half:], nf, 1))
        packed_im = jnp.where(low, pltpu.roll(imag[:half], nf, 1), imag[half:])
        sp_v[t] = jnp.concatenate([packed_re, packed_im], axis=0).astype(BF16)

    def forward(step, carry):
        for i in range(2):
            spectrum(2 * step + i)
        return carry

    sums = sq_v[...]
    high = sums.astype(BF16)
    rest = (sums - high.astype(F32)).astype(BF16)
    spot = lax.broadcasted_iota(jnp.int32, (px, B * SC), 0) // BLK_PX
    group = lax.broadcasted_iota(jnp.int32, (px, B * SC), 1) // SC
    fold = jnp.where(spot == group, 1.0 / (BLK_PX * BLK_PX), 0.0).astype(BF16)
    both = jnp.dot(jnp.concatenate([high, rest], axis=0), fold, preferred_element_type=F32)
    density = both[: tiles * B] + both[tiles * B :]
    row_of = lax.broadcasted_iota(jnp.int32, (tiles * B, LANES), 0)
    lane_of = lax.broadcasted_iota(jnp.int32, (tiles * B, LANES), 1)
    cell_rows = jnp.zeros((tiles * B, LANES), jnp.int32)
    classes, cells, slots = [], [], []
    for t in range(tiles):
        classes.append(class_ref[t])
        cells.append(cell_ref[t])
        rank = jnp.int32(0)
        for before in range(t):
            rank = rank + jnp.where(classes[before] == classes[t], 1, 0)
        slots.append(classes[t] * CAP + rank)
        cell_rows = jnp.where(row_of // B == t, cells[t], cell_rows)
    strip_rows = cell_rows // SC
    wanted_column = jnp.where(lane_of == cell_rows - strip_rows * SC, 1.0, 0.0)[:, :SC]
    wanted_row = jnp.concatenate(
        [jnp.where(lane_of + first == strip_rows * B + row_of % B, 1.0, 0.0) for first in range(0, strips * B, LANES)],
        axis=1)
    exact = dict(precision=lax.Precision.HIGHEST, preferred_element_type=F32)
    downs = jnp.dot(wanted_row, down_ref[...], **exact)
    alongs = jnp.dot(wanted_column, along_ref[...], **exact)
    share = lax.dot_general(downs, density * alongs, (((0,), (0,)), ((), ())), **exact)[:strips]
    share = share[:, :LANES] + share[:, LANES:]
    share = share + pltpu.roll(share, 2 * SC, 1)
    share = share + pltpu.roll(share, SC, 1)
    row_at = lax.broadcasted_iota(jnp.int32, (tiles, LANES), 0)
    lane_at = lax.broadcasted_iota(jnp.int32, (tiles, LANES), 1)
    info = jnp.zeros((tiles, LANES), F32)
    for t in range(tiles):
        entry = jnp.where(lane_at == 0, cells[t], slots[t]).astype(F32)
        info = jnp.where(row_at == t, entry, info)
    hs_v[:strips] = share
    hs_v[strips:] = info
    hr_v[0] = hs_v[...]

    pl.semaphore_wait(barrier, n_focus - 1 + n_tile - 1)

    def h_copy(o):
        return pltpu.make_async_remote_copy(
            src_ref=hs_v, dst_ref=hr_v.at[o], send_sem=h_send.at[o], recv_sem=h_recv.at[o],
            device_id=(my_t, ahead(o)), device_id_type=MESH)

    def z_copy(o):
        return pltpu.make_async_remote_copy(
            src_ref=zs_v, dst_ref=zr_v.at[o], send_sem=z_send.at[o], recv_sem=z_recv.at[o],
            device_id=(above(o), my_f), device_id_type=MESH)

    def s_copy(o):
        return pltpu.make_async_remote_copy(
            src_ref=out_v.at[o], dst_ref=in_v.at[o], send_sem=s_send.at[o], recv_sem=s_recv.at[o],
            device_id=(my_t, ahead(o)), device_id_type=MESH)

    def r_copy(o):
        return pltpu.make_async_remote_copy(
            src_ref=lit_v.at[o], dst_ref=ret_ref.at[my_f], send_sem=r_send.at[o], recv_sem=r_recv.at[o],
            device_id=(my_t, behind(o)), device_id_type=MESH)

    for o in range(1, n_focus):
        h_copy(o).start()

    tables[2].wait()
    tables[3].wait()
    lax.fori_loop(0, tiles // 2, forward, 0)

    for o in range(1, n_focus):
        h_copy(o).wait_recv()
    subtotal = hr_v[0, :strips]
    for o in range(1, n_focus):
        subtotal = subtotal + hr_v[o, :strips]
    zs_v[...] = subtotal
    for o in range(1, n_tile):
        z_copy(o).start()
    slot_tiles = [jnp.full((8, LANES), slots[t], jnp.int32) for t in range(tiles)]
    for o in range(n_focus):
        target = in_v if o == 0 else out_v
        for j in range(CAP):
            name = ahead(o) * CAP + j
            chosen = jnp.zeros((2 * nf // 16, 8, 2 * nf), F32)
            for t in range(tiles):
                chosen = jnp.where((slot_tiles[t] == name)[None], sp_v[t].astype(F32).reshape(chosen.shape), chosen)
            target[o, j] = chosen.reshape(nf, 2 * nf).astype(BF16)
        if o > 0:
            s_copy(o).start()

    tables[4].wait()

    def lay(k, carry):
        for b in range(half):
            w_v[k, pl.ds(b, 4, stride=half), :] = raw_v[k, :, b * 2 * nf : (b + 1) * 2 * nf].astype(F32)
        return carry

    lax.fori_loop(0, ker, lay, 0)
    for o in range(1, n_tile):
        z_copy(o).wait_recv()
    heights = subtotal
    for o in range(1, n_tile):
        heights = heights + zr_v[o]
    average = jnp.sum(heights, keepdims=True) / (strips * LANES)
    names = hr_v[:, strips:, :].reshape(n_focus * tiles, LANES)
    cell_col, slot_col = names[:, 0:1], names[:, 1:2]
    strip_col = jnp.floor(cell_col / SC)
    column_col = cell_col - strip_col * SC
    picked = jnp.zeros((n_focus * tiles, LANES), F32)
    for r in range(strips):
        picked = jnp.where(strip_col == r, heights[r : r + 1], picked)
    lane = lax.broadcasted_iota(jnp.int32, picked.shape, 1).astype(F32)
    own = jnp.sum(jnp.where(lane == column_col, picked, 0.0), axis=1, keepdims=True)
    defocus = GAIN_SCALE * (own - average) - center_ref[my_f]
    for j in range(CAP):
        here = slot_col == (my_f * CAP + j).astype(F32)
        kept = jnp.broadcast_to(jnp.where(here, defocus, 0.0), picked.shape)
        shift_v[j] = jnp.sum(kept.reshape(n_focus, tiles, LANES), axis=1)

    def filtered(o, j, m):
        d = shift_v[j, pl.ds(o, 1), :]
        spec = in_v[o, j].astype(F32)
        sr, si = spec[:half], spec[half:]
        rows = []
        for k in (m, m + 1):
            w = [w_v[k, i * half : (i + 1) * half, :] for i in range(4)]
            kr, ki = w[0] + d * w[2], w[1] + d * w[3]
            rows.append(jnp.concatenate([kr * sr - ki * si, kr * si + ki * sr], axis=1).astype(BF16))
        return jnp.concatenate(rows, axis=0)

    def image(now, after):
        across = jnp.dot(fil_v[now], whole(right_ref), preferred_element_type=F32).astype(BF16)
        left = left_ref[...]
        total = jnp.zeros((Q, Q), F32)
        for k in range(0, ker, 2):
            fil_v[1 - now, k * half : (k + 2) * half, :] = filtered(*after, k)
            sides = []
            for m in (k, k + 1):
                rows = across[m * half : (m + 1) * half]
                sides.append(jnp.concatenate([rows[:, i * Q : (i + 1) * Q] for i in range(4)], axis=0))
            fields = jnp.dot(left, jnp.concatenate(sides, axis=1), preferred_element_type=F32)
            power = fields * fields
            total = total + ((power[:Q, :Q] + power[Q:, :Q]) + (power[:Q, Q:] + power[Q:, Q:]))
        return (total / ker).astype(BF16)

    own_copy = pltpu.make_async_copy(lit_v.at[0], ret_ref.at[my_f], own_sem)
    tables[5].wait()
    tables[6].wait()
    s_copy(1).wait_recv()
    for k in range(0, ker, 2):
        fil_v[0, k * half : (k + 2) * half, :] = filtered(1, 0, k)

    def serve(step, carry):
        o = lax.rem(step + 1, n_focus)
        following = lax.rem(step + 2, n_focus)
        for j in range(CAP):
            if j == CAP - 1:
                @pl.when(step < n_focus - 2)
                def _():
                    s_copy(following).wait_recv()
            lit_v[o, j] = image(j % 2, (o, j + 1) if j < CAP - 1 else (following, 0))

        @pl.when(o != 0)
        def _():
            r_copy(o).start()

        return carry

    lax.fori_loop(0, n_focus, serve, 0)
    own_copy.start()
    own_copy.wait()
    for o in range(1, n_focus):
        r_copy(o).wait_recv()
    for o in range(1, n_focus):
        h_copy(o).wait_send()
        s_copy(o).wait_send()
        r_copy(o).wait_send()
    for o in range(1, n_tile):
        z_copy(o).wait_send()


def resist_kernel(class_ref, lit_hbm, wide_ref, tall_ref, out_ref, lit_v, out_v, in_sem, out_sem):
    tiles = out_v.shape[0]

    def fetch(t):
        own = class_ref[t]
        rank = jnp.int32(0)
        for b in range(t):
            rank = rank + jnp.where(class_ref[b] == own, 1, 0)
        return pltpu.make_async_copy(lit_hbm.at[own * CAP + rank], lit_v.at[t], in_sem.at[t])

    def leave(t):
        return pltpu.make_async_copy(out_v.at[t], out_ref.at[t], out_sem.at[t])

    copies = [fetch(t) for t in range(tiles)]
    for copy in copies:
        copy.start()
    for t in range(tiles):
        copies[t].wait()
        half_way = jnp.dot(lit_v[t], whole(wide_ref), preferred_element_type=F32).astype(BF16)
        out_v[t] = jnp.dot(tall_ref[...], half_way, preferred_element_type=F32).astype(BF16)
        leave(t).start()
    for t in range(tiles):
        leave(t).wait()


def per_device(n_tile, n_focus, mask_tiles, class_of_tile, cell_of_tile, kernels, class_center):
    tiles, px, _ = mask_tiles.shape
    _, ker, parts, area = kernels.shape
    nf = int(round(area ** 0.5))
    half = nf // 2
    strips = SR_DEV * n_tile
    wave_x, wave_y = wave_tables(nf, px)
    right, left = image_tables(nf)
    down, along = height_tables(strips)
    resist = resist_table(px)
    tables = [wave_x, in_columns(wave_y), in_columns(right), left, down, along]
    classes = class_of_tile.reshape(tiles)
    smem = pl.BlockSpec(memory_space=pltpu.SMEM)
    vmem = pl.BlockSpec(memory_space=pltpu.VMEM)
    anywhere = pl.BlockSpec(memory_space=pl.ANY)
    dma = pltpu.SemaphoreType.DMA
    slots = n_focus * CAP
    row_work = slots * ker * (half * 4 * nf * 4 * Q + 2 * Q * 2 * nf * Q)
    returned = pl.pallas_call(
        functools.partial(imaging_kernel, n_tile, n_focus, strips, ker, nf),
        out_shape=jax.ShapeDtypeStruct((n_focus, CAP, Q, Q), BF16),
        in_specs=[anywhere, smem, smem, smem] + [anywhere] * 7,
        out_specs=anywhere,
        scratch_shapes=[
            pltpu.VMEM((tiles, px, px), BF16),
            pltpu.VMEM((tiles * B, px), F32),
            pltpu.VMEM((tiles, nf, 2 * nf), BF16),
            pltpu.VMEM((n_focus, CAP, nf, 2 * nf), BF16),
            pltpu.VMEM((n_focus, CAP, nf, 2 * nf), BF16),
            pltpu.VMEM((strips + tiles, LANES), F32),
            pltpu.VMEM((n_focus, strips + tiles, LANES), F32),
            pltpu.VMEM((strips, LANES), F32),
            pltpu.VMEM((n_tile, strips, LANES), F32),
            pltpu.VMEM((CAP, n_focus, LANES), F32),
            pltpu.VMEM((n_focus, CAP, Q, Q), BF16),
            pltpu.VMEM((ker, parts, area), BF16),
            pltpu.VMEM((ker, parts * half, 2 * nf), F32),
            pltpu.VMEM((2, ker * half, 4 * nf), BF16),
        ] + [pltpu.VMEM(table.shape, table.dtype) for table in tables] + [
            dma((tiles,)),
            dma((n_focus,)), dma((n_focus,)),
            dma((n_tile,)), dma((n_tile,)),
            dma((n_focus,)), dma((n_focus,)),
            dma((n_focus,)), dma((n_focus,)),
            dma,
            dma((len(tables) + 1,)),
        ],
        compiler_params=pltpu.CompilerParams(
            collective_id=0, has_side_effects=True, vmem_limit_bytes=56 * 1024 * 1024),
        cost_estimate=pl.CostEstimate(flops=2 * row_work, bytes_accessed=8 * 1024 * 1024, transcendentals=0),
        name="imaging",
    )(mask_tiles, classes, cell_of_tile, class_center, kernels, *tables)
    return pl.pallas_call(
        resist_kernel,
        out_shape=jax.ShapeDtypeStruct((tiles, px, px), BF16),
        in_specs=[smem, anywhere, vmem, vmem],
        out_specs=anywhere,
        scratch_shapes=[
            pltpu.VMEM((tiles, Q, Q), BF16), pltpu.VMEM((tiles, px, px), BF16), dma((tiles,)), dma((tiles,))],
        compiler_params=pltpu.CompilerParams(vmem_limit_bytes=56 * 1024 * 1024),
        cost_estimate=pl.CostEstimate(
            flops=2 * tiles * Q * px * (Q + px), bytes_accessed=2 * tiles * px * px, transcendentals=0),
        name="resist",
    )(classes, returned.reshape(slots, Q, Q), in_columns(resist.T), resist)


def solution(mesh):
    placed = (
        P(("tile", "focus"), None, None),
        P(("tile", "focus"), None),
        P(("tile", "focus")),
        P("focus", None, None, None),
        P(),
    )
    return jax.shard_map(
        functools.partial(per_device, mesh.shape["tile"], mesh.shape["focus"]),
        mesh=mesh,
        in_specs=placed,
        out_specs=P(("tile", "focus"), None, None),
        check_vma=False,
    )
```

```python
import functools

import jax
import jax.numpy as jnp
import ml_dtypes
import numpy as np
from jax import lax
from jax.experimental import pallas as pl
from jax.experimental.pallas import tpu as pltpu
from jax.sharding import PartitionSpec as P

BLK_PX = 64
CAP = 2
SC = 32
SR_DEV = 4
Q = 128
B = 8
REACH = 64
GAIN_SCALE = 50.0
LANES = 128
MESH = pl.DeviceIdType.MESH
F32 = jnp.float32
BF16 = jnp.bfloat16


def trig(freq_count, length):
    frequency = np.arange(freq_count) - freq_count // 2
    phases = np.mod(frequency[:, None] * np.arange(length)[None, :], length) * (2.0 * np.pi / length)
    return np.cos(phases), np.sin(phases)


def as_bf16(table):
    return np.asarray(table, np.float32).astype(ml_dtypes.bfloat16)


def in_columns(table):
    return np.stack(np.split(table, table.shape[1] // LANES, axis=1))


def whole(ref):
    return jnp.concatenate([ref[i] for i in range(ref.shape[0])], axis=1)


def wave_tables(nf, pixels):
    c, s = trig(nf, pixels)
    across = np.concatenate([c, s], axis=0).T
    down = np.concatenate([c[0::2], c[1::2], s[0::2], s[1::2]], axis=0)
    return as_bf16(across), as_bf16(down)


def image_tables(nf):
    c, s = trig(nf, Q)
    zero = np.zeros_like(c)
    right = np.block([[c, s, zero, zero], [zero, zero, c, s], [-s, c, zero, zero], [zero, zero, -s, c]])
    full = np.block([[c, s], [-s, c]]).T
    order = np.concatenate([np.arange(0, nf, 2), nf + np.arange(0, nf, 2), np.arange(1, nf, 2), nf + np.arange(1, nf, 2)])
    return as_bf16(right), as_bf16(full[:, order])


def resist_table(pixels):
    cp, sp = trig(Q, pixels)
    cq, sq = trig(Q, Q)
    frequency = np.arange(Q) - Q // 2
    weight = np.exp(-0.5 * (frequency * (4.0 / Q)) ** 2)[:, None]
    return as_bf16(((cp * weight).T @ cq + (sp * weight).T @ sq) / Q)


def spread_table(extent):
    places = np.arange(extent)
    weight = np.exp(-np.abs(places[:, None] - places[None, :]) / REACH)
    return weight / weight.sum(axis=1, keepdims=True)


def height_tables(strips):
    down = spread_table(strips * B).reshape(strips, B, strips * B).mean(axis=1).T
    down = np.pad(down, ((0, 0), (0, LANES - strips)))
    along = spread_table(SC * B).reshape(SC * B, SC, B).mean(axis=2).reshape(SC, B * SC)
    return down.astype(np.float32), along.astype(np.float32)


def imaging_kernel(
    n_tile, n_focus, strips, ker, nf,
    mask_hbm, class_ref, cell_ref, center_ref, w_hbm, wave_x_hbm, wave_y_hbm, right_hbm, left_hbm, down_hbm, along_hbm,
    ret_ref,
    mask_v, sq_v, sp_v, out_v, in_v, hs_v, hr_v, zs_v, zr_v, shift_v, lit_v, raw_v, w_v, fil_v,
    wave_x, wave_y, right_ref, left_ref, down_ref, along_ref,
    mask_sem, h_send, h_recv, z_send, z_recv, s_send, s_recv, r_send, r_recv, own_sem, table_sem,
):
    my_t, my_f = lax.axis_index("tile"), lax.axis_index("focus")
    tiles, px, _ = mask_v.shape
    half = nf // 2

    def ahead(o):
        return lax.rem(my_f + o, n_focus)

    def behind(o):
        return lax.rem(my_f + n_focus - o, n_focus)

    def above(o):
        return lax.rem(my_t + o, n_tile)

    def mask_copy(t):
        return pltpu.make_async_copy(mask_hbm.at[t], mask_v.at[t], mask_sem.at[t])

    fetched = [
        (down_hbm, down_ref), (along_hbm, along_ref), (wave_x_hbm, wave_x), (wave_y_hbm, wave_y),
        (w_hbm.at[0], raw_v), (right_hbm, right_ref), (left_hbm, left_ref)]
    tables = [pltpu.make_async_copy(src, dst, table_sem.at[i]) for i, (src, dst) in enumerate(fetched)]

    for t in range(tiles):
        mask_copy(t).start()
    for table in tables:
        table.start()
    barrier = pltpu.get_barrier_semaphore()
    for o in range(1, n_focus):
        pl.semaphore_signal(barrier, inc=1, device_id=(my_t, ahead(o)), device_id_type=MESH)
    for o in range(1, n_tile):
        pl.semaphore_signal(barrier, inc=1, device_id=(above(o), my_f), device_id_type=MESH)

    def squares(t, carry):
        mask_copy(t).wait()
        wide = mask_v[t].astype(F32)
        sq_v[pl.ds(pl.multiple_of(t * B, B), B), :] = jnp.sum((wide * wide).reshape(B, BLK_PX, px), axis=1)
        return carry

    lax.fori_loop(0, tiles, squares, 0)
    tables[0].wait()
    tables[1].wait()

    def spectrum(t):
        projected = jnp.dot(mask_v[t], wave_x[...], preferred_element_type=F32).astype(BF16)
        raw = jnp.dot(whole(wave_y), projected, preferred_element_type=F32)
        top, bottom = raw[:nf], pltpu.roll(raw[nf:], nf, 1)
        real, imag = (top - bottom) / px, -(top + bottom) / px
        low = lax.broadcasted_iota(jnp.int32, (half, 2 * nf), 1) < nf
        packed_re = jnp.where(low, real[:half], pltpu.roll(real[half:], nf, 1))
        packed_im = jnp.where(low, pltpu.roll(imag[:half], nf, 1), imag[half:])
        sp_v[t] = jnp.concatenate([packed_re, packed_im], axis=0).astype(BF16)

    def forward(step, carry):
        for i in range(2):
            spectrum(2 * step + i)
        return carry

    sums = sq_v[...]
    high = sums.astype(BF16)
    rest = (sums - high.astype(F32)).astype(BF16)
    spot = lax.broadcasted_iota(jnp.int32, (px, B * SC), 0) // BLK_PX
    group = lax.broadcasted_iota(jnp.int32, (px, B * SC), 1) // SC
    fold = jnp.where(spot == group, 1.0 / (BLK_PX * BLK_PX), 0.0).astype(BF16)
    both = jnp.dot(jnp.concatenate([high, rest], axis=0), fold, preferred_element_type=F32)
    density = both[: tiles * B] + both[tiles * B :]
    row_of = lax.broadcasted_iota(jnp.int32, (tiles * B, LANES), 0)
    lane_of = lax.broadcasted_iota(jnp.int32, (tiles * B, LANES), 1)
    cell_rows = jnp.zeros((tiles * B, LANES), jnp.int32)
    classes, cells, slots = [], [], []
    for t in range(tiles):
        classes.append(class_ref[t])
        cells.append(cell_ref[t])
        rank = jnp.int32(0)
        for before in range(t):
            rank = rank + jnp.where(classes[before] == classes[t], 1, 0)
        slots.append(classes[t] * CAP + rank)
        cell_rows = jnp.where(row_of // B == t, cells[t], cell_rows)
    strip_rows = cell_rows // SC
    wanted_column = jnp.where(lane_of == cell_rows - strip_rows * SC, 1.0, 0.0)[:, :SC]
    wanted_row = jnp.concatenate(
        [jnp.where(lane_of + first == strip_rows * B + row_of % B, 1.0, 0.0) for first in range(0, strips * B, LANES)],
        axis=1)
    exact = dict(precision=lax.Precision.HIGHEST, preferred_element_type=F32)
    downs = jnp.dot(wanted_row, down_ref[...], **exact)
    alongs = jnp.dot(wanted_column, along_ref[...], **exact)
    share = lax.dot_general(downs, density * alongs, (((0,), (0,)), ((), ())), **exact)[:strips]
    share = share[:, :LANES] + share[:, LANES:]
    share = share + pltpu.roll(share, 2 * SC, 1)
    share = share + pltpu.roll(share, SC, 1)
    row_at = lax.broadcasted_iota(jnp.int32, (tiles, LANES), 0)
    lane_at = lax.broadcasted_iota(jnp.int32, (tiles, LANES), 1)
    info = jnp.zeros((tiles, LANES), F32)
    for t in range(tiles):
        entry = jnp.where(lane_at == 0, cells[t], slots[t]).astype(F32)
        info = jnp.where(row_at == t, entry, info)
    hs_v[:strips] = share
    hs_v[strips:] = info
    hr_v[0] = hs_v[...]

    pl.semaphore_wait(barrier, n_focus - 1 + n_tile - 1)

    def h_copy(o):
        return pltpu.make_async_remote_copy(
            src_ref=hs_v, dst_ref=hr_v.at[o], send_sem=h_send.at[o], recv_sem=h_recv.at[o],
            device_id=(my_t, ahead(o)), device_id_type=MESH)

    def z_copy(o):
        return pltpu.make_async_remote_copy(
            src_ref=zs_v, dst_ref=zr_v.at[o], send_sem=z_send.at[o], recv_sem=z_recv.at[o],
            device_id=(above(o), my_f), device_id_type=MESH)

    def s_copy(o):
        return pltpu.make_async_remote_copy(
            src_ref=out_v.at[o], dst_ref=in_v.at[o], send_sem=s_send.at[o], recv_sem=s_recv.at[o],
            device_id=(my_t, ahead(o)), device_id_type=MESH)

    def r_copy(o):
        return pltpu.make_async_remote_copy(
            src_ref=lit_v.at[o], dst_ref=ret_ref.at[my_f], send_sem=r_send.at[o], recv_sem=r_recv.at[o],
            device_id=(my_t, behind(o)), device_id_type=MESH)

    for o in range(1, n_focus):
        h_copy(o).start()

    tables[2].wait()
    tables[3].wait()
    lax.fori_loop(0, tiles // 2, forward, 0)

    for o in range(1, n_focus):
        h_copy(o).wait_recv()
    subtotal = hr_v[0, :strips]
    for o in range(1, n_focus):
        subtotal = subtotal + hr_v[o, :strips]
    zs_v[...] = subtotal
    for o in range(1, n_tile):
        z_copy(o).start()
    slot_tiles = [jnp.full((8, LANES), slots[t], jnp.int32) for t in range(tiles)]
    for o in range(n_focus):
        target = in_v if o == 0 else out_v
        for j in range(CAP):
            name = ahead(o) * CAP + j
            chosen = jnp.zeros((2 * nf // 16, 8, 2 * nf), F32)
            for t in range(tiles):
                chosen = jnp.where((slot_tiles[t] == name)[None], sp_v[t].astype(F32).reshape(chosen.shape), chosen)
            target[o, j] = chosen.reshape(nf, 2 * nf).astype(BF16)
        if o > 0:
            s_copy(o).start()

    tables[4].wait()

    def lay(k, carry):
        for b in range(half):
            w_v[k, pl.ds(b, 4, stride=half), :] = raw_v[k, :, b * 2 * nf : (b + 1) * 2 * nf].astype(F32)
        return carry

    lax.fori_loop(0, ker, lay, 0)
    for o in range(1, n_tile):
        z_copy(o).wait_recv()
    heights = subtotal
    for o in range(1, n_tile):
        heights = heights + zr_v[o]
    average = jnp.sum(heights, keepdims=True) / (strips * LANES)
    names = hr_v[:, strips:, :].reshape(n_focus * tiles, LANES)
    cell_col, slot_col = names[:, 0:1], names[:, 1:2]
    strip_col = jnp.floor(cell_col / SC)
    column_col = cell_col - strip_col * SC
    picked = jnp.zeros((n_focus * tiles, LANES), F32)
    for r in range(strips):
        picked = jnp.where(strip_col == r, heights[r : r + 1], picked)
    lane = lax.broadcasted_iota(jnp.int32, picked.shape, 1).astype(F32)
    own = jnp.sum(jnp.where(lane == column_col, picked, 0.0), axis=1, keepdims=True)
    defocus = GAIN_SCALE * (own - average) - center_ref[my_f]
    for j in range(CAP):
        here = slot_col == (my_f * CAP + j).astype(F32)
        kept = jnp.broadcast_to(jnp.where(here, defocus, 0.0), picked.shape)
        shift_v[j] = jnp.sum(kept.reshape(n_focus, tiles, LANES), axis=1)

    def filtered(o, j, m):
        d = shift_v[j, pl.ds(o, 1), :]
        spec = in_v[o, j].astype(F32)
        sr, si = spec[:half], spec[half:]
        rows = []
        for k in (m, m + 1):
            w = [w_v[k, i * half : (i + 1) * half, :] for i in range(4)]
            kr, ki = w[0] + d * w[2], w[1] + d * w[3]
            rows.append(jnp.concatenate([kr * sr - ki * si, kr * si + ki * sr], axis=1).astype(BF16))
        return jnp.concatenate(rows, axis=0)

    def image(now, after):
        across = jnp.dot(fil_v[now], whole(right_ref), preferred_element_type=F32).astype(BF16)
        left = left_ref[...]
        total = jnp.zeros((Q, Q), F32)
        for first in range(0, ker, 4):
            sides = []
            for m in range(first, min(first + 4, ker)):
                if m % 2 == 0:
                    fil_v[1 - now, m * half : (m + 2) * half, :] = filtered(*after, m)
                rows = across[m * half : (m + 1) * half]
                sides.append(jnp.concatenate([rows[:, i * Q : (i + 1) * Q] for i in range(4)], axis=0))
            fields = jnp.dot(left, jnp.concatenate(sides, axis=1), preferred_element_type=F32)
            power = fields * fields
            for i in range(len(sides)):
                total = total + (power[:Q, i * Q : (i + 1) * Q] + power[Q:, i * Q : (i + 1) * Q])
        return (total / ker).astype(BF16)

    own_copy = pltpu.make_async_copy(lit_v.at[0], ret_ref.at[my_f], own_sem)
    tables[5].wait()
    tables[6].wait()
    s_copy(1).wait_recv()
    for k in range(0, ker, 2):
        fil_v[0, k * half : (k + 2) * half, :] = filtered(1, 0, k)

    def serve(step, carry):
        o = lax.rem(step + 1, n_focus)
        following = lax.rem(step + 2, n_focus)
        for j in range(CAP):
            if j == CAP - 1:
                @pl.when(step < n_focus - 2)
                def _():
                    s_copy(following).wait_recv()
            lit_v[o, j] = image(j % 2, (o, j + 1) if j < CAP - 1 else (following, 0))

        @pl.when(o != 0)
        def _():
            r_copy(o).start()

        return carry

    lax.fori_loop(0, n_focus, serve, 0)
    own_copy.start()
    own_copy.wait()
    for o in range(1, n_focus):
        r_copy(o).wait_recv()
    for o in range(1, n_focus):
        h_copy(o).wait_send()
        s_copy(o).wait_send()
        r_copy(o).wait_send()
    for o in range(1, n_tile):
        z_copy(o).wait_send()


def resist_kernel(class_ref, lit_hbm, wide_hbm, tall_hbm, out_ref, wide_ref, tall_ref, lit_v, out_v, sem, in_sem, out_sem):
    tiles = out_v.shape[0]

    def fetch(t):
        own = class_ref[t]
        rank = jnp.int32(0)
        for b in range(t):
            rank = rank + jnp.where(class_ref[b] == own, 1, 0)
        return pltpu.make_async_copy(lit_hbm.at[own * CAP + rank], lit_v.at[t], in_sem.at[t])

    def leave(t):
        return pltpu.make_async_copy(out_v.at[t], out_ref.at[t], out_sem.at[t])

    wide_copy = pltpu.make_async_copy(wide_hbm, wide_ref, sem.at[0])
    tall_copy = pltpu.make_async_copy(tall_hbm, tall_ref, sem.at[1])
    copies = [wide_copy] + [fetch(t) for t in range(tiles)] + [tall_copy]
    for copy in copies:
        copy.start()
    for copy in copies:
        copy.wait()
    wide, tall = whole(wide_ref), tall_ref[...]
    half_way = jnp.dot(lit_v[...].reshape(tiles * Q, Q), wide, preferred_element_type=F32).astype(BF16)
    for t in range(tiles):
        out_v[t] = jnp.dot(tall, half_way[t * Q : (t + 1) * Q], preferred_element_type=F32).astype(BF16)
        leave(t).start()
    for t in range(tiles):
        leave(t).wait()


def per_device(n_tile, n_focus, mask_tiles, class_of_tile, cell_of_tile, kernels, class_center):
    tiles, px, _ = mask_tiles.shape
    _, ker, parts, area = kernels.shape
    nf = int(round(area ** 0.5))
    half = nf // 2
    strips = SR_DEV * n_tile
    wave_x, wave_y = wave_tables(nf, px)
    right, left = image_tables(nf)
    down, along = height_tables(strips)
    resist = resist_table(px)
    wide = in_columns(resist.T)
    tables = [wave_x, in_columns(wave_y), in_columns(right), left, down, along]
    classes = class_of_tile.reshape(tiles)
    smem = pl.BlockSpec(memory_space=pltpu.SMEM)
    anywhere = pl.BlockSpec(memory_space=pl.ANY)
    dma = pltpu.SemaphoreType.DMA
    slots = n_focus * CAP
    row_work = slots * ker * (half * 4 * nf * 4 * Q + 2 * Q * 2 * nf * Q)
    returned = pl.pallas_call(
        functools.partial(imaging_kernel, n_tile, n_focus, strips, ker, nf),
        out_shape=jax.ShapeDtypeStruct((n_focus, CAP, Q, Q), BF16),
        in_specs=[anywhere, smem, smem, smem] + [anywhere] * 7,
        out_specs=anywhere,
        scratch_shapes=[
            pltpu.VMEM((tiles, px, px), BF16),
            pltpu.VMEM((tiles * B, px), F32),
            pltpu.VMEM((tiles, nf, 2 * nf), BF16),
            pltpu.VMEM((n_focus, CAP, nf, 2 * nf), BF16),
            pltpu.VMEM((n_focus, CAP, nf, 2 * nf), BF16),
            pltpu.VMEM((strips + tiles, LANES), F32),
            pltpu.VMEM((n_focus, strips + tiles, LANES), F32),
            pltpu.VMEM((strips, LANES), F32),
            pltpu.VMEM((n_tile, strips, LANES), F32),
            pltpu.VMEM((CAP, n_focus, LANES), F32),
            pltpu.VMEM((n_focus, CAP, Q, Q), BF16),
            pltpu.VMEM((ker, parts, area), BF16),
            pltpu.VMEM((ker, parts * half, 2 * nf), F32),
            pltpu.VMEM((2, ker * half, 4 * nf), BF16),
        ] + [pltpu.VMEM(table.shape, table.dtype) for table in tables] + [
            dma((tiles,)),
            dma((n_focus,)), dma((n_focus,)),
            dma((n_tile,)), dma((n_tile,)),
            dma((n_focus,)), dma((n_focus,)),
            dma((n_focus,)), dma((n_focus,)),
            dma,
            dma((len(tables) + 1,)),
        ],
        compiler_params=pltpu.CompilerParams(
            collective_id=0, has_side_effects=True, vmem_limit_bytes=56 * 1024 * 1024),
        cost_estimate=pl.CostEstimate(flops=2 * row_work, bytes_accessed=8 * 1024 * 1024, transcendentals=0),
        name="imaging",
    )(mask_tiles, classes, cell_of_tile, class_center, kernels, *tables)
    return pl.pallas_call(
        resist_kernel,
        out_shape=jax.ShapeDtypeStruct((tiles, px, px), BF16),
        in_specs=[smem, anywhere, anywhere, anywhere],
        out_specs=anywhere,
        scratch_shapes=[
            pltpu.VMEM(wide.shape, BF16), pltpu.VMEM(resist.shape, BF16),
            pltpu.VMEM((tiles, Q, Q), BF16), pltpu.VMEM((tiles, px, px), BF16),
            dma((2,)), dma((tiles,)), dma((tiles,))],
        compiler_params=pltpu.CompilerParams(vmem_limit_bytes=56 * 1024 * 1024),
        cost_estimate=pl.CostEstimate(
            flops=2 * tiles * Q * px * (Q + px), bytes_accessed=2 * tiles * px * px, transcendentals=0),
        name="resist",
    )(classes, returned.reshape(slots, Q, Q), wide, resist)


def solution(mesh):
    placed = (
        P(("tile", "focus"), None, None),
        P(("tile", "focus"), None),
        P(("tile", "focus")),
        P("focus", None, None, None),
        P(),
    )
    return jax.shard_map(
        functools.partial(per_device, mesh.shape["tile"], mesh.shape["focus"]),
        mesh=mesh,
        in_specs=placed,
        out_specs=P(("tile", "focus"), None, None),
        check_vma=False,
    )
```

```python
import functools

import jax
import jax.numpy as jnp
import ml_dtypes
import numpy as np
from jax import lax
from jax.experimental import pallas as pl
from jax.experimental.pallas import tpu as pltpu
from jax.sharding import PartitionSpec as P

BLK_PX = 64
CAP = 2
SC = 32
SR_DEV = 4
Q = 128
B = 8
REACH = 64
GAIN_SCALE = 50.0
LANES = 128
MESH = pl.DeviceIdType.MESH
F32 = jnp.float32
BF16 = jnp.bfloat16


def trig(freq_count, length):
    frequency = np.arange(freq_count) - freq_count // 2
    phases = np.mod(frequency[:, None] * np.arange(length)[None, :], length) * (2.0 * np.pi / length)
    return np.cos(phases), np.sin(phases)


def as_bf16(table):
    return np.asarray(table, np.float32).astype(ml_dtypes.bfloat16)


def in_columns(table):
    return np.stack(np.split(table, table.shape[1] // LANES, axis=1))


def whole(ref):
    return jnp.concatenate([ref[i] for i in range(ref.shape[0])], axis=1)


def wave_tables(nf, pixels):
    c, s = trig(nf, pixels)
    across = np.concatenate([c, s], axis=0).T
    down = np.concatenate([c[0::2], c[1::2], s[0::2], s[1::2]], axis=0)
    return as_bf16(across), as_bf16(down)


def image_tables(nf):
    c, s = trig(nf, Q)
    zero = np.zeros_like(c)
    right = np.block([[c, s, zero, zero], [zero, zero, c, s], [-s, c, zero, zero], [zero, zero, -s, c]])
    full = np.block([[c, s], [-s, c]]).T
    order = np.concatenate([np.arange(0, nf, 2), nf + np.arange(0, nf, 2), np.arange(1, nf, 2), nf + np.arange(1, nf, 2)])
    return as_bf16(right), as_bf16(full[:, order])


def resist_table(pixels):
    cp, sp = trig(Q, pixels)
    cq, sq = trig(Q, Q)
    frequency = np.arange(Q) - Q // 2
    weight = np.exp(-0.5 * (frequency * (4.0 / Q)) ** 2)[:, None]
    return as_bf16(((cp * weight).T @ cq + (sp * weight).T @ sq) / Q)


def spread_table(extent):
    places = np.arange(extent)
    weight = np.exp(-np.abs(places[:, None] - places[None, :]) / REACH)
    return weight / weight.sum(axis=1, keepdims=True)


def height_tables(strips):
    down = spread_table(strips * B).reshape(strips, B, strips * B).mean(axis=1).T
    down = np.pad(down, ((0, 0), (0, LANES - strips)))
    along = spread_table(SC * B).reshape(SC * B, SC, B).mean(axis=2).reshape(SC, B * SC)
    return down.astype(np.float32), along.astype(np.float32)


def imaging_kernel(
    n_tile, n_focus, strips, ker, nf,
    mask_hbm, class_ref, cell_ref, center_ref, w_hbm, wave_x_hbm, wave_y_hbm, right_hbm, left_hbm, down_hbm, along_hbm,
    ret_ref,
    mask_v, sq_v, sp_v, out_v, in_v, hs_v, hr_v, zs_v, zr_v, shift_v, lit_v, raw_v, w_v, fil_v, xs_v,
    wave_x, wave_y, right_ref, left_ref, down_ref, along_ref,
    mask_sem, h_send, h_recv, z_send, z_recv, s_send, s_recv, r_send, r_recv, own_sem, table_sem,
):
    my_t, my_f = lax.axis_index("tile"), lax.axis_index("focus")
    tiles, px, _ = mask_v.shape
    half = nf // 2

    def ahead(o):
        return lax.rem(my_f + o, n_focus)

    def behind(o):
        return lax.rem(my_f + n_focus - o, n_focus)

    def above(o):
        return lax.rem(my_t + o, n_tile)

    def mask_copy(t):
        return pltpu.make_async_copy(mask_hbm.at[t], mask_v.at[t], mask_sem.at[t])

    fetched = [
        (down_hbm, down_ref), (along_hbm, along_ref), (wave_x_hbm, wave_x), (wave_y_hbm, wave_y),
        (w_hbm.at[0], raw_v), (right_hbm, right_ref), (left_hbm, left_ref)]
    tables = [pltpu.make_async_copy(src, dst, table_sem.at[i]) for i, (src, dst) in enumerate(fetched)]

    for t in range(tiles):
        mask_copy(t).start()
    for table in tables:
        table.start()
    barrier = pltpu.get_barrier_semaphore()
    for o in range(1, n_focus):
        pl.semaphore_signal(barrier, inc=1, device_id=(my_t, ahead(o)), device_id_type=MESH)
    for o in range(1, n_tile):
        pl.semaphore_signal(barrier, inc=1, device_id=(above(o), my_f), device_id_type=MESH)

    def squares(t, carry):
        mask_copy(t).wait()
        wide = mask_v[t].astype(F32)
        sq_v[pl.ds(pl.multiple_of(t * B, B), B), :] = jnp.sum((wide * wide).reshape(B, BLK_PX, px), axis=1)
        return carry

    lax.fori_loop(0, tiles, squares, 0)
    tables[0].wait()
    tables[1].wait()

    batch = 4 if tiles % 4 == 0 else 1

    def forward(step, carry):
        masks = mask_v[pl.ds(step * batch, batch)].reshape(batch * px, px)
        projected = jnp.dot(masks, wave_x[...], preferred_element_type=F32).astype(BF16)
        beside = jnp.concatenate([projected[i * px : (i + 1) * px] for i in range(batch)], axis=1)
        raws = jnp.dot(whole(wave_y), beside, preferred_element_type=F32)
        low = lax.broadcasted_iota(jnp.int32, (half, 2 * nf), 1) < nf
        for i in range(batch):
            raw = raws[:, i * 2 * nf : (i + 1) * 2 * nf]
            top, bottom = raw[:nf], pltpu.roll(raw[nf:], nf, 1)
            real, imag = (top - bottom) / px, -(top + bottom) / px
            packed_re = jnp.where(low, real[:half], pltpu.roll(real[half:], nf, 1))
            packed_im = jnp.where(low, pltpu.roll(imag[:half], nf, 1), imag[half:])
            sp_v[step * batch + i] = jnp.concatenate([packed_re, packed_im], axis=0).astype(BF16)
        return carry

    sums = sq_v[...]
    high = sums.astype(BF16)
    rest = (sums - high.astype(F32)).astype(BF16)
    spot = lax.broadcasted_iota(jnp.int32, (px, B * SC), 0) // BLK_PX
    group = lax.broadcasted_iota(jnp.int32, (px, B * SC), 1) // SC
    fold = jnp.where(spot == group, 1.0 / (BLK_PX * BLK_PX), 0.0).astype(BF16)
    both = jnp.dot(jnp.concatenate([high, rest], axis=0), fold, preferred_element_type=F32)
    density = both[: tiles * B] + both[tiles * B :]
    row_of = lax.broadcasted_iota(jnp.int32, (tiles * B, LANES), 0)
    lane_of = lax.broadcasted_iota(jnp.int32, (tiles * B, LANES), 1)
    cell_rows = jnp.zeros((tiles * B, LANES), jnp.int32)
    classes, cells, slots = [], [], []
    for t in range(tiles):
        classes.append(class_ref[t])
        cells.append(cell_ref[t])
        rank = jnp.int32(0)
        for before in range(t):
            rank = rank + jnp.where(classes[before] == classes[t], 1, 0)
        slots.append(classes[t] * CAP + rank)
        cell_rows = jnp.where(row_of // B == t, cells[t], cell_rows)
    strip_rows = cell_rows // SC
    wanted_column = jnp.where(lane_of == cell_rows - strip_rows * SC, 1.0, 0.0)[:, :SC]
    wanted_row = jnp.concatenate(
        [jnp.where(lane_of + first == strip_rows * B + row_of % B, 1.0, 0.0) for first in range(0, strips * B, LANES)],
        axis=1)
    exact = dict(precision=lax.Precision.HIGHEST, preferred_element_type=F32)
    downs = jnp.dot(wanted_row, down_ref[...], **exact)
    alongs = jnp.dot(wanted_column, along_ref[...], **exact)
    share = lax.dot_general(downs, density * alongs, (((0,), (0,)), ((), ())), **exact)[:strips]
    share = share[:, :LANES] + share[:, LANES:]
    share = share + pltpu.roll(share, 2 * SC, 1)
    share = share + pltpu.roll(share, SC, 1)
    row_at = lax.broadcasted_iota(jnp.int32, (tiles, LANES), 0)
    lane_at = lax.broadcasted_iota(jnp.int32, (tiles, LANES), 1)
    info = jnp.zeros((tiles, LANES), F32)
    for t in range(tiles):
        entry = jnp.where(lane_at == 0, cells[t], slots[t]).astype(F32)
        info = jnp.where(row_at == t, entry, info)
    hs_v[:strips] = share
    hs_v[strips:] = info
    hr_v[0] = hs_v[...]

    pl.semaphore_wait(barrier, n_focus - 1 + n_tile - 1)

    def h_copy(o):
        return pltpu.make_async_remote_copy(
            src_ref=hs_v, dst_ref=hr_v.at[o], send_sem=h_send.at[o], recv_sem=h_recv.at[o],
            device_id=(my_t, ahead(o)), device_id_type=MESH)

    def z_copy(o):
        return pltpu.make_async_remote_copy(
            src_ref=zs_v, dst_ref=zr_v.at[o], send_sem=z_send.at[o], recv_sem=z_recv.at[o],
            device_id=(above(o), my_f), device_id_type=MESH)

    def s_copy(o):
        return pltpu.make_async_remote_copy(
            src_ref=out_v.at[o], dst_ref=in_v.at[o], send_sem=s_send.at[o], recv_sem=s_recv.at[o],
            device_id=(my_t, ahead(o)), device_id_type=MESH)

    def r_copy(o):
        return pltpu.make_async_remote_copy(
            src_ref=lit_v.at[o], dst_ref=ret_ref.at[my_f], send_sem=r_send.at[o], recv_sem=r_recv.at[o],
            device_id=(my_t, behind(o)), device_id_type=MESH)

    for o in range(1, n_focus):
        h_copy(o).start()

    tables[2].wait()
    tables[3].wait()
    lax.fori_loop(0, tiles // batch, forward, 0)

    for o in range(1, n_focus):
        h_copy(o).wait_recv()
    subtotal = hr_v[0, :strips]
    for o in range(1, n_focus):
        subtotal = subtotal + hr_v[o, :strips]
    zs_v[...] = subtotal
    for o in range(1, n_tile):
        z_copy(o).start()
    slot_tiles = [jnp.full((8, LANES), slots[t], jnp.int32) for t in range(tiles)]
    for o in range(n_focus):
        target = in_v if o == 0 else out_v
        for j in range(CAP):
            name = ahead(o) * CAP + j
            chosen = jnp.zeros((2 * nf // 16, 8, 2 * nf), F32)
            for t in range(tiles):
                chosen = jnp.where((slot_tiles[t] == name)[None], sp_v[t].astype(F32).reshape(chosen.shape), chosen)
            target[o, j] = chosen.reshape(nf, 2 * nf).astype(BF16)
        if o > 0:
            s_copy(o).start()

    tables[4].wait()

    def lay(k, carry):
        for b in range(half):
            w_v[k, pl.ds(b, 4, stride=half), :] = raw_v[k, :, b * 2 * nf : (b + 1) * 2 * nf].astype(F32)
        return carry

    lax.fori_loop(0, ker, lay, 0)
    for o in range(1, n_tile):
        z_copy(o).wait_recv()
    heights = subtotal
    for o in range(1, n_tile):
        heights = heights + zr_v[o]
    average = jnp.sum(heights, keepdims=True) / (strips * LANES)
    names = hr_v[:, strips:, :].reshape(n_focus * tiles, LANES)
    cell_col, slot_col = names[:, 0:1], names[:, 1:2]
    strip_col = jnp.floor(cell_col / SC)
    column_col = cell_col - strip_col * SC
    picked = jnp.zeros((n_focus * tiles, LANES), F32)
    for r in range(strips):
        picked = jnp.where(strip_col == r, heights[r : r + 1], picked)
    lane = lax.broadcasted_iota(jnp.int32, picked.shape, 1).astype(F32)
    own = jnp.sum(jnp.where(lane == column_col, picked, 0.0), axis=1, keepdims=True)
    defocus = GAIN_SCALE * (own - average) - center_ref[my_f]
    for j in range(CAP):
        here = slot_col == (my_f * CAP + j).astype(F32)
        kept = jnp.broadcast_to(jnp.where(here, defocus, 0.0), picked.shape)
        shift_v[j] = jnp.sum(kept.reshape(n_focus, tiles, LANES), axis=1)

    def filtered(o, j, m):
        d = shift_v[j, pl.ds(o, 1), :]
        spec = in_v[o, j].astype(F32)
        sr, si = spec[:half], spec[half:]
        rows = []
        for k in (m, m + 1):
            w = [w_v[k, i * half : (i + 1) * half, :] for i in range(4)]
            kr, ki = w[0] + d * w[2], w[1] + d * w[3]
            rows.append(jnp.concatenate([kr * sr - ki * si, kr * si + ki * sr], axis=1).astype(BF16))
        return jnp.concatenate(rows, axis=0)

    def sideways(which):
        xs_v[which] = jnp.dot(fil_v[which], whole(right_ref), preferred_element_type=F32).astype(BF16)

    def image(now, after):
        sideways(1 - now)
        left = left_ref[...]
        total = jnp.zeros((Q, Q), F32)
        for first in range(0, ker, 4):
            sides = []
            for m in range(first, min(first + 4, ker)):
                if m % 2 == 0:
                    fil_v[now, m * half : (m + 2) * half, :] = filtered(*after, m)
                sides.append(jnp.concatenate(
                    [xs_v[now, m * half : (m + 1) * half, i * Q : (i + 1) * Q] for i in range(4)], axis=0))
            fields = jnp.dot(left, jnp.concatenate(sides, axis=1), preferred_element_type=F32)
            power = fields * fields
            for i in range(len(sides)):
                total = total + (power[:Q, i * Q : (i + 1) * Q] + power[Q:, i * Q : (i + 1) * Q])
        return (total / ker).astype(BF16)

    own_copy = pltpu.make_async_copy(lit_v.at[0], ret_ref.at[my_f], own_sem)
    tables[5].wait()
    tables[6].wait()
    s_copy(1).wait_recv()
    for j in range(CAP):
        for k in range(0, ker, 2):
            fil_v[j, k * half : (k + 2) * half, :] = filtered(1, j, k)
    sideways(0)

    def serve(step, carry):
        o = lax.rem(step + 1, n_focus)
        following = lax.rem(step + 2, n_focus)

        @pl.when(step < n_focus - 2)
        def _():
            s_copy(following).wait_recv()

        for j in range(CAP):
            lit_v[o, j] = image(j, (following, j))

        @pl.when(o != 0)
        def _():
            r_copy(o).start()

        return carry

    lax.fori_loop(0, n_focus, serve, 0)
    own_copy.start()
    own_copy.wait()
    for o in range(1, n_focus):
        r_copy(o).wait_recv()
    for o in range(1, n_focus):
        h_copy(o).wait_send()
        s_copy(o).wait_send()
        r_copy(o).wait_send()
    for o in range(1, n_tile):
        z_copy(o).wait_send()


def resist_kernel(class_ref, lit_hbm, wide_hbm, tall_hbm, out_ref, wide_ref, tall_ref, lit_v, out_v, sem, in_sem, out_sem):
    tiles = out_v.shape[0]

    def fetch(t):
        own = class_ref[t]
        rank = jnp.int32(0)
        for b in range(t):
            rank = rank + jnp.where(class_ref[b] == own, 1, 0)
        return pltpu.make_async_copy(lit_hbm.at[own * CAP + rank], lit_v.at[t], in_sem.at[t])

    def leave(t):
        return pltpu.make_async_copy(out_v.at[t], out_ref.at[t], out_sem.at[t])

    wide_copy = pltpu.make_async_copy(wide_hbm, wide_ref, sem.at[0])
    tall_copy = pltpu.make_async_copy(tall_hbm, tall_ref, sem.at[1])
    copies = [wide_copy] + [fetch(t) for t in range(tiles)] + [tall_copy]
    for copy in copies:
        copy.start()
    for copy in copies:
        copy.wait()
    wide, tall = whole(wide_ref), tall_ref[...]
    half_way = jnp.dot(lit_v[...].reshape(tiles * Q, Q), wide, preferred_element_type=F32).astype(BF16)
    for t in range(tiles):
        out_v[t] = jnp.dot(tall, half_way[t * Q : (t + 1) * Q], preferred_element_type=F32).astype(BF16)
        leave(t).start()
    for t in range(tiles):
        leave(t).wait()


def per_device(n_tile, n_focus, mask_tiles, class_of_tile, cell_of_tile, kernels, class_center):
    tiles, px, _ = mask_tiles.shape
    _, ker, parts, area = kernels.shape
    nf = int(round(area ** 0.5))
    half = nf // 2
    strips = SR_DEV * n_tile
    wave_x, wave_y = wave_tables(nf, px)
    right, left = image_tables(nf)
    down, along = height_tables(strips)
    resist = resist_table(px)
    wide = in_columns(resist.T)
    tables = [wave_x, in_columns(wave_y), in_columns(right), left, down, along]
    classes = class_of_tile.reshape(tiles)
    smem = pl.BlockSpec(memory_space=pltpu.SMEM)
    anywhere = pl.BlockSpec(memory_space=pl.ANY)
    dma = pltpu.SemaphoreType.DMA
    slots = n_focus * CAP
    row_work = slots * ker * (half * 4 * nf * 4 * Q + 2 * Q * 2 * nf * Q)
    returned = pl.pallas_call(
        functools.partial(imaging_kernel, n_tile, n_focus, strips, ker, nf),
        out_shape=jax.ShapeDtypeStruct((n_focus, CAP, Q, Q), BF16),
        in_specs=[anywhere, smem, smem, smem] + [anywhere] * 7,
        out_specs=anywhere,
        scratch_shapes=[
            pltpu.VMEM((tiles, px, px), BF16),
            pltpu.VMEM((tiles * B, px), F32),
            pltpu.VMEM((tiles, nf, 2 * nf), BF16),
            pltpu.VMEM((n_focus, CAP, nf, 2 * nf), BF16),
            pltpu.VMEM((n_focus, CAP, nf, 2 * nf), BF16),
            pltpu.VMEM((strips + tiles, LANES), F32),
            pltpu.VMEM((n_focus, strips + tiles, LANES), F32),
            pltpu.VMEM((strips, LANES), F32),
            pltpu.VMEM((n_tile, strips, LANES), F32),
            pltpu.VMEM((CAP, n_focus, LANES), F32),
            pltpu.VMEM((n_focus, CAP, Q, Q), BF16),
            pltpu.VMEM((ker, parts, area), BF16),
            pltpu.VMEM((ker, parts * half, 2 * nf), F32),
            pltpu.VMEM((CAP, ker * half, 4 * nf), BF16),
            pltpu.VMEM((CAP, ker * half, 4 * Q), BF16),
        ] + [pltpu.VMEM(table.shape, table.dtype) for table in tables] + [
            dma((tiles,)),
            dma((n_focus,)), dma((n_focus,)),
            dma((n_tile,)), dma((n_tile,)),
            dma((n_focus,)), dma((n_focus,)),
            dma((n_focus,)), dma((n_focus,)),
            dma,
            dma((len(tables) + 1,)),
        ],
        compiler_params=pltpu.CompilerParams(
            collective_id=0, has_side_effects=True, vmem_limit_bytes=56 * 1024 * 1024),
        cost_estimate=pl.CostEstimate(flops=2 * row_work, bytes_accessed=8 * 1024 * 1024, transcendentals=0),
        name="imaging",
    )(mask_tiles, classes, cell_of_tile, class_center, kernels, *tables)
    return pl.pallas_call(
        resist_kernel,
        out_shape=jax.ShapeDtypeStruct((tiles, px, px), BF16),
        in_specs=[smem, anywhere, anywhere, anywhere],
        out_specs=anywhere,
        scratch_shapes=[
            pltpu.VMEM(wide.shape, BF16), pltpu.VMEM(resist.shape, BF16),
            pltpu.VMEM((tiles, Q, Q), BF16), pltpu.VMEM((tiles, px, px), BF16),
            dma((2,)), dma((tiles,)), dma((tiles,))],
        compiler_params=pltpu.CompilerParams(vmem_limit_bytes=56 * 1024 * 1024),
        cost_estimate=pl.CostEstimate(
            flops=2 * tiles * Q * px * (Q + px), bytes_accessed=2 * tiles * px * px, transcendentals=0),
        name="resist",
    )(classes, returned.reshape(slots, Q, Q), wide, resist)


def solution(mesh):
    placed = (
        P(("tile", "focus"), None, None),
        P(("tile", "focus"), None),
        P(("tile", "focus")),
        P("focus", None, None, None),
        P(),
    )
    return jax.shard_map(
        functools.partial(per_device, mesh.shape["tile"], mesh.shape["focus"]),
        mesh=mesh,
        in_specs=placed,
        out_specs=P(("tile", "focus"), None, None),
        check_vma=False,
    )
```
